256 devices in a mesh: row: 16 (over y, x_lo, core), col: 16 (over x_hi, z).
Axes of the slice: x: 4 (x_hi: 2, x_lo: 2; x = x_hi * 2 + x_lo), y: 4, z: 8, core: 2. Of those that a mesh axis runs over, the one named last changes fastest.
Arguments:
- tokens: bfloat16 [4096, 6144], P('row', 'col'), may hold values from -6 to 6
- gate_weight_blocks: bfloat16 [2816, 128, 128], P(('row', 'col')), may hold values from -0.125 to 0.125
- up_weight_blocks: bfloat16 [2816, 128, 128], P(('row', 'col')), may hold values from -0.125 to 0.125
- block_row: int32 [2816], P(('row', 'col')), may hold values from -1 to 47, as said below
- block_col: int32 [2816], P(('row', 'col')), may hold values from -1 to 191, as said below
- grad_hidden: bfloat16 [4096, 24576], P('row', 'col'), may hold values from -6 to 6
Outputs:
- hidden: bfloat16 [4096, 24576], P('row', 'col')
- grad_tokens: bfloat16 [4096, 6144], P('row', 'col')
The draws below stay inside these ranges and needn't reach their ends.
Inputs may be any that keep to these rules, and one draw needn't show every extreme that they name: Slot s of the device at index r of row and c of col lies at position (r * 16 + c) * 11 + s. Such a slot is empty (block_row and block_col both -1) or names a block with block_row in [r * 3, (r + 1) * 3) and block_col in [c * 12, (c + 1) * 12); the live slots of a device come first, at least one, and name distinct blocks; in every draw some device has all 11 slots live. `block_col`: empty exactly where block_row is empty, as described there.
All inputs are finite; a program needn't handle non-finite values.
Results may differ from the reference program's by a relative error of at most 0.0049.
Values may be sent and summed in bfloat16 or wider, within the bound.
No kernel may reach another device: no remote copies, remote signals or barrier semaphores. Data moves between devices by JAX's collectives and lax.ppermute only.
A program may use at most 64 MiB of HBM per device.

```python
import jax
import jax.numpy as jnp
from jax import lax

MODEL_WIDTH = 6144
FF = 24576
BLOCK_SIDE = 128
SLOTS = 11
TOKENS = 4096
GRID_ROWS = 16
GRID_COLS = 16
KR = 3
KC = 12
SLOT_NUMBER = 2816


def slot_pattern(key):
    tile_total = GRID_ROWS * GRID_COLS
    count_key, full_key, order_key = jax.random.split(key, 3)
    counts = jax.random.randint(count_key, (tile_total,), max(SLOTS * 3 // 4, 1), SLOTS + 1)
    chosen = jax.random.randint(full_key, (), 0, tile_total)
    tile_ids = jnp.arange(tile_total)
    counts = jnp.where(tile_ids == chosen, SLOTS, counts)
    order_keys = jax.random.split(order_key, tile_total)
    orders = jax.vmap(lambda sub_key: jax.random.permutation(sub_key, KR * KC))(order_keys)[:, :SLOTS]
    live_slot = jnp.arange(SLOTS)[None, :] < counts[:, None]
    row_ids = (tile_ids // GRID_COLS)[:, None] * KR + orders // KC
    col_ids = (tile_ids % GRID_COLS)[:, None] * KC + orders % KC
    row_ids = jnp.where(live_slot, row_ids, -1).reshape(-1).astype(jnp.int32)
    col_ids = jnp.where(live_slot, col_ids, -1).reshape(-1).astype(jnp.int32)
    return (row_ids, col_ids)


def draw_block_row(key, part):
    return slot_pattern(key)[0]


def draw_block_col(key, part):
    return slot_pattern(key)[1]


def level_of(rng, extent, cuts, least, top_value):
    def one(dim, blocks):
        heights = jax.random.uniform(jax.random.fold_in(jax.random.fold_in(rng, 6), dim), (blocks,), jnp.float32, least / len(cuts), top_value / len(cuts))
        return jnp.repeat(jnp.exp(heights), extent[dim] // blocks).reshape((-1,) + (1,) * (len(extent) - dim - 1))

    loudness = one(*cuts[0])
    for cut in cuts[1:]:
        loudness = loudness * one(*cut)
    return loudness


def centred(stream_key, dims, spread, reach, cuts=(), held_as=jnp.bfloat16):
    drawn = spread * jax.random.normal(stream_key, dims, jnp.float32)
    if cuts:
        drawn = drawn * level_of(stream_key, dims, cuts, -0.22, 0.18)
    return jnp.clip(drawn, -reach, reach).astype(held_as)


def setup_inputs(seed: int = 0) -> dict:
    streams_of = jax.random.split(jax.random.key(seed), 7)
    return {
        "tokens": centred(streams_of[0], (TOKENS, MODEL_WIDTH), 1.0, 6.0, ((0, 16), (1, 16))),
        "gate_weight_blocks": centred(streams_of[1], (SLOT_NUMBER, BLOCK_SIDE, BLOCK_SIDE), (MODEL_WIDTH * 3 // 10) ** -0.5, 0.125, ((0, 256),)),
        "up_weight_blocks": centred(streams_of[2], (SLOT_NUMBER, BLOCK_SIDE, BLOCK_SIDE), (MODEL_WIDTH * 3 // 10) ** -0.5, 0.125, ((0, 256),)),
        "block_row": draw_block_row(jax.random.fold_in(streams_of[6], 71), 0),
        "block_col": draw_block_col(jax.random.fold_in(streams_of[6], 71), 0),
        "grad_hidden": centred(streams_of[5], (TOKENS, FF), 1.0, 6.0, ((0, 16), (1, 16))),
    }


def reference(tokens, gate_weight_blocks, up_weight_blocks, block_row, block_col, grad_hidden):
    token_count = tokens.shape[0]
    row_count = MODEL_WIDTH // BLOCK_SIDE
    col_total = FF // BLOCK_SIDE
    group_total = gate_weight_blocks.shape[0] // SLOTS
    token_blocks = tokens.astype(jnp.float32).reshape(token_count, row_count, BLOCK_SIDE)
    stacked = (gate_weight_blocks.reshape(group_total, SLOTS, BLOCK_SIDE, BLOCK_SIDE),
               up_weight_blocks.reshape(group_total, SLOTS, BLOCK_SIDE, BLOCK_SIDE),
               block_row.reshape(group_total, SLOTS),
               block_col.reshape(group_total, SLOTS))

    def forward_step(running, group_item):
        gate_group, up_group, row_group, col_group = group_item
        taken_rows = jnp.take(token_blocks, jnp.maximum(row_group, 0).astype(jnp.int32), axis=1)
        gate_partial_terms = jnp.einsum("tmk,mkc->tmc", taken_rows, gate_group.astype(jnp.float32), precision=lax.Precision.HIGHEST)
        up_terms = jnp.einsum("tmk,mkc->tmc", taken_rows, up_group.astype(jnp.float32), precision=lax.Precision.HIGHEST)
        target = jnp.where(col_group < 0, col_total, col_group).astype(jnp.int32)
        gate_sum = running[0].at[:, target].add(gate_partial_terms, mode="drop")
        up_sum = running[1].at[:, target].add(up_terms, mode="drop")
        return (gate_sum, up_sum), None

    zero_cols = jnp.zeros((token_count, col_total, BLOCK_SIDE), jnp.float32)
    (gate_act, up_act), _ = lax.scan(forward_step, (zero_cols, zero_cols), stacked)
    gate_act = gate_act.reshape(token_count, FF)
    up_act = up_act.reshape(token_count, FF)
    sigmoid_gate = jax.nn.sigmoid(gate_act)
    silu_gate = gate_act * sigmoid_gate
    hidden = (silu_gate * up_act).astype(jnp.bfloat16)
    upstream = grad_hidden.astype(jnp.float32)
    grad_gate = (upstream * up_act * sigmoid_gate * (1.0 + gate_act * (1.0 - sigmoid_gate))).astype(jnp.bfloat16)
    grad_up = (upstream * silu_gate).astype(jnp.bfloat16)
    gate_grad_blocks = grad_gate.astype(jnp.float32).reshape(token_count, col_total, BLOCK_SIDE)
    up_grad_blocks = grad_up.astype(jnp.float32).reshape(token_count, col_total, BLOCK_SIDE)

    def backward_update(running, group_item):
        gate_group, up_group, row_group, col_group = group_item
        local_cols = jnp.maximum(col_group, 0).astype(jnp.int32)
        gate_taken = jnp.take(gate_grad_blocks, local_cols, axis=1)
        up_selected = jnp.take(up_grad_blocks, local_cols, axis=1)
        terms = jnp.einsum("tmc,mkc->tmk", gate_taken, gate_group.astype(jnp.float32), precision=lax.Precision.HIGHEST)
        terms = terms + jnp.einsum("tmc,mkc->tmk", up_selected, up_group.astype(jnp.float32), precision=lax.Precision.HIGHEST)
        target = jnp.where(row_group < 0, row_count, row_group).astype(jnp.int32)
        return running.at[:, target].add(terms, mode="drop"), None

    zero_rows = jnp.zeros((token_count, row_count, BLOCK_SIDE), jnp.float32)
    grad_sum, _ = lax.scan(backward_update, zero_rows, stacked)
    grad_tokens = grad_sum.reshape(token_count, MODEL_WIDTH).astype(jnp.bfloat16)
    return hidden, grad_tokens
```

```python
import jax
import jax.numpy as jnp
from jax import lax
from jax.experimental import pallas as pl
from jax.experimental.pallas import tpu as pltpu
from jax.sharding import Mesh, PartitionSpec as P

AXES = ("y", "x_lo", "core", "x_hi", "z")
ROW = ("y", "x_lo", "core")
COL = ("x_hi", "z")
SIZES = {"y": 4, "x_lo": 2, "core": 2, "x_hi": 2, "z": 8}
VMEM_LIMIT = 56 * 1024 * 1024


def shift(value, axis, step):
    size = SIZES[axis]
    return lax.ppermute(value, axis, [(i, (i + step) % size) for i in range(size)])


def forward_kernel(order, rows, cols, x_ref, w_ref, up_ref, hidden_ref, grads_ref, acc):
    step = pl.program_id(0)
    slots = w_ref.shape[1]
    side = w_ref.shape[2]
    col_count = grads_ref.shape[0]
    base = order[step] * slots

    @pl.when(step == 0)
    def _():
        acc[...] = jnp.zeros_like(acc)

    for slot in range(slots):
        row = rows[base + slot]
        col = cols[base + slot]
        taken = x_ref[0, :, pl.ds(pl.multiple_of(jnp.minimum(row, 2) * side, side), side)]
        acc[col] += jnp.dot(taken, w_ref[0, slot], preferred_element_type=jnp.float32)

    @pl.when(step == pl.num_programs(0) - 1)
    def _():
        for j in range(col_count):
            gate = acc[j, :, :side]
            up = acc[j, :, side:]
            sig = 1.0 / (1.0 + jnp.exp(-gate))
            silu = gate * sig
            hidden_ref[:, j * side:(j + 1) * side] = (silu * up).astype(jnp.bfloat16)
            upstream = up_ref[:, j * side:(j + 1) * side].astype(jnp.float32)
            grads_ref[j, :, :side] = (
                upstream * up * sig * (1.0 + gate * (1.0 - sig))
            ).astype(jnp.bfloat16)
            grads_ref[j, :, side:] = (upstream * silu).astype(jnp.bfloat16)


def forward(order, rows, cols, x, w, upstream):
    tiles, tokens, span = x.shape
    slots, side, pair = w.shape[1:]
    width = upstream.shape[1]
    col_count = width // side
    grid_spec = pltpu.PrefetchScalarGridSpec(
        num_scalar_prefetch=3,
        grid=(tiles,),
        in_specs=[
            pl.BlockSpec((1, tokens, span), lambda i, order, rows, cols: (i, 0, 0)),
            pl.BlockSpec((1, slots, side, pair), lambda i, order, rows, cols: (order[i], 0, 0, 0)),
            pl.BlockSpec((tokens, width), lambda i, order, rows, cols: (0, 0)),
        ],
        out_specs=[
            pl.BlockSpec((tokens, width), lambda i, order, rows, cols: (0, 0)),
            pl.BlockSpec((col_count, tokens, pair), lambda i, order, rows, cols: (0, 0, 0)),
        ],
        scratch_shapes=[pltpu.VMEM((col_count + 1, tokens, pair), jnp.float32)],
    )
    return pl.pallas_call(
        forward_kernel,
        grid_spec=grid_spec,
        out_shape=[
            jax.ShapeDtypeStruct((tokens, width), jnp.bfloat16),
            jax.ShapeDtypeStruct((col_count, tokens, pair), jnp.bfloat16),
        ],
        compiler_params=pltpu.CompilerParams(vmem_limit_bytes=VMEM_LIMIT),
        cost_estimate=pl.CostEstimate(
            flops=2 * tiles * slots * tokens * side * pair,
            bytes_accessed=2 * (x.size + w.size + 5 * upstream.size),
            transcendentals=2 * upstream.size,
        ),
        name="forward",
    )(order, rows, cols, x, w, upstream)


def backward_kernel(order, rows, cols, grads_ref, w_ref, out_ref, acc):
    step = pl.program_id(0)
    slots = w_ref.shape[1]
    side = w_ref.shape[2]
    col_count = grads_ref.shape[0]
    base = order[step] * slots
    acc[...] = jnp.zeros_like(acc)
    for slot in range(slots):
        row = rows[base + slot]
        col = jnp.minimum(cols[base + slot], col_count - 1)
        acc[row] += lax.dot_general(
            grads_ref[col],
            w_ref[0, slot],
            (((1,), (1,)), ((), ())),
            preferred_element_type=jnp.float32,
        )
    for j in range(out_ref.shape[2] // side):
        out_ref[0, :, j * side:(j + 1) * side] = acc[j].astype(out_ref.dtype)


def backward(order, rows, cols, grads, w, dtype):
    steps = order.shape[0]
    col_count, tokens, pair = grads.shape
    slots, side = w.shape[1:3]
    tile_rows = 3
    span = tile_rows * side
    grid_spec = pltpu.PrefetchScalarGridSpec(
        num_scalar_prefetch=3,
        grid=(steps,),
        in_specs=[
            pl.BlockSpec((col_count, tokens, pair), lambda i, order, rows, cols: (0, 0, 0)),
            pl.BlockSpec((1, slots, side, pair), lambda i, order, rows, cols: (order[i], 0, 0, 0)),
        ],
        out_specs=pl.BlockSpec((1, tokens, span), lambda i, order, rows, cols: (i, 0, 0)),
        scratch_shapes=[pltpu.VMEM((tile_rows + 1, tokens, side), jnp.float32)],
    )
    return pl.pallas_call(
        backward_kernel,
        grid_spec=grid_spec,
        out_shape=jax.ShapeDtypeStruct((steps, tokens, span), dtype),
        compiler_params=pltpu.CompilerParams(vmem_limit_bytes=VMEM_LIMIT),
        cost_estimate=pl.CostEstimate(
            flops=2 * steps * slots * tokens * side * pair,
            bytes_accessed=2 * (grads.size + steps * slots * side * pair + 2 * steps * tokens * span),
            transcendentals=0,
        ),
        name="backward",
    )(order, rows, cols, grads, w)


def gather_tokens(tokens, home):
    x_hi, z = home
    across = shift(tokens, "x_hi", 1)
    chunks = []
    for value, hi, far in ((tokens, x_hi, 1), (across, 1 - x_hi, -1)):
        chunks.append((value, hi * 8 + z))
        for step in (1, -1):
            moving = value
            for hop in range(1, 4 + (step == far)):
                moving = shift(moving, "z", step)
                chunks.append((moving, hi * 8 + (z - step * hop) % 8))
    return chunks


def on_device(tokens, gate_blocks, up_blocks, block_row, block_col, upstream):
    x_hi, z = lax.axis_index("x_hi"), lax.axis_index("z")
    bf16, f32 = jnp.bfloat16, jnp.float32
    slots, side = gate_blocks.shape[:2]
    pairs = jnp.concatenate([gate_blocks, up_blocks], axis=2)
    w = lax.all_gather(pairs, ROW, axis=0, tiled=True).reshape(-1, slots, side, 2 * side)
    chunks = gather_tokens(tokens, (x_hi, z))
    x = jnp.stack([value for value, _ in chunks])
    order = jnp.stack([index for _, index in chunks]).astype(jnp.int32)

    ids = jnp.concatenate([
        jnp.where(block_row < 0, 3, block_row % 3),
        jnp.where(block_row < 0, 12, block_col % 12),
    ])
    ids = lax.all_gather(ids, ROW, axis=0, tiled=True).reshape(-1, 2, slots)
    rows, cols = ids[:, 0].reshape(-1), ids[:, 1].reshape(-1)

    hidden, grads = forward(order, rows, cols, x, w, upstream)

    def terms(offsets):
        group = [hi * 8 + (z + dz) % 8 for dz in offsets for hi in (0, 1)]
        return backward(jnp.stack(group).astype(jnp.int32), rows, cols, grads, w, f32)

    part = terms((4,)).astype(bf16)
    plus, minus = shift(part[0], "z", 1), shift(part[1], "z", -1)
    part = terms((3, -3))
    plus = jnp.stack([part[0] + plus, part[1]]).astype(bf16)
    minus = jnp.stack([part[2], part[3] + minus]).astype(bf16)
    for distance in (2, 1):
        plus, minus = shift(plus, "z", 1), shift(minus, "z", -1)
        part = terms((distance, -distance))
        plus = (part[:2] + plus).astype(bf16)
        minus = (part[2:] + minus).astype(bf16)
    plus, minus = shift(plus, "z", 1), shift(minus, "z", -1)
    total = terms((0,)) + plus + minus
    mine = jnp.where(x_hi == 0, total[0], total[1])
    other = jnp.where(x_hi == 0, total[1], total[0]).astype(bf16)
    grad_tokens = (mine + shift(other, "x_hi", 1)).astype(bf16)
    return hidden, grad_tokens


def solution(mesh):
    fine = Mesh(mesh.devices.reshape([SIZES[a] for a in AXES]), AXES)
    both = P(ROW, COL)
    return jax.shard_map(
        on_device,
        mesh=fine,
        in_specs=(both, P(ROW + COL, None, None), P(ROW + COL, None, None), P(ROW + COL), P(ROW + COL), both),
        out_specs=(both, both),
        check_vma=False,
    )
```

```python
import functools

import jax
import jax.numpy as jnp
import numpy as np
from jax import lax
from jax.experimental import pallas as pl
from jax.experimental.pallas import tpu as pltpu
from jax.sharding import Mesh, PartitionSpec as P

AXES = ("y", "x_lo", "core", "x_hi", "z")
ROW = ("y", "x_lo", "core")
COL = ("x_hi", "z")
SIZES = {"y": 4, "x_lo": 2, "core": 2, "x_hi": 2, "z": 8}
SIDE = 128
EARLY_CHUNKS = 10
ORDER = (4, 3, -3, 2, -2, 1, -1, 0)
VMEM_LIMIT = 10 * 1024 * 1024
ON_CHIP = pl.BlockSpec(memory_space=pltpu.VMEM)
ANYWHERE = pl.BlockSpec(memory_space=pl.ANY)
SCALARS = pl.BlockSpec(memory_space=pltpu.SMEM)


TILES = [
    (0, 0, 0), (0, 0, 1), (-1, 0, 0), (-1, 0, 1), (0, 1, 0), (-2, 0, 0), (1, 1, 0), (-3, 0, 0), (-1, 1, 0),
    (0, 1, 1), (-2, 0, 1), (1, 1, 1), (-3, 0, 1), (-1, 1, 1), (2, 1, 0), (2, 1, 1),
]
CHUNKS = [(hi, dz) for dz in (0, -1, 1, -2, 2, -3, 3, 4) for hi in (0, 1)]


def plans():
    table = []
    for y, x_lo, core, x_hi, z in np.ndindex(*(SIZES[a] for a in AXES)):
        tiles = []
        for step, other_x, other_core in TILES:
            c = (core + other_core) % 2
            tiles.append((y + step * (1 - 2 * c)) % 4 * 4 + (x_lo + other_x) % 2 * 2 + c)
        chunks = [(x_hi + other) % 2 * 8 + (z + dz) % 8 for other, dz in CHUNKS]
        columns = [(x_hi + other) % 2 * 8 + (z + dz) % 8 for other in (1, 0) for dz in ORDER]
        table.append([chunks.index(k) for k in tiles] + [tiles.index(k) for k in columns])
    return np.array(table, np.int32)


PLANS = plans()


def shift(value, axis, step):
    size = SIZES[axis]
    return lax.ppermute(value, axis, [(i, (i + step) % size) for i in range(size)])


def turn(value, sign):
    pairs = []
    for y in range(4):
        for core, step in ((0, sign), (1, -sign)):
            pairs.append((y * 2 + core, (y + step) % 4 * 2 + core))
    return lax.ppermute(value, ("y", "core"), pairs)


def slot_of(ref, tile, slot):
    return ref[tile, slot * SIDE:(slot + 1) * SIDE]


def load(parts, whole, sems, first=0):
    copies = []
    for number, part in enumerate(parts):
        if len(part.shape) == len(whole.shape):
            place, first = whole.at[pl.ds(first, part.shape[0])], first + part.shape[0]
        else:
            place, first = whole.at[first], first + 1
        copy = pltpu.make_async_copy(part, place, sems.at[number])
        copy.start()
        copies.append(copy)
    return copies


def add_tile(tile, pick, names, x_ref, w_ref, acc):
    slots = names.shape[1] // 2
    for slot in range(slots):
        row = jnp.minimum(names[tile, slot], 2)
        col = names[tile, slots + slot]
        taken = x_ref[pick[tile], :, pl.ds(pl.multiple_of(row * SIDE, SIDE), SIDE)]
        acc[col] += jnp.dot(taken, slot_of(w_ref, tile, slot), preferred_element_type=jnp.float32)


def early_kernel(n_x, n_w, pick, names, *refs):
    x_parts, w_parts = refs[:n_x], refs[n_x:n_x + n_w]
    x_ref, w_ref, acc, x_sems, w_sems = refs[n_x + n_w:]
    x_copies = load(x_parts, x_ref, x_sems)
    w_copies = load(w_parts, w_ref, w_sems)
    acc[...] = jnp.zeros_like(acc)
    for copy in x_copies:
        copy.wait()

    def tile_step(tile, carry):
        pltpu.make_async_copy(w_parts[0], w_ref.at[tile], w_sems.at[tile]).wait()

        @pl.when(pick[tile] < EARLY_CHUNKS)
        def _():
            add_tile(tile, pick, names, x_ref, w_ref, acc)

        return carry

    lax.fori_loop(0, len(w_copies), tile_step, 0)


def late_kernel(n_x, n_w, pick, names, up_ref, *refs):
    x_parts, w_parts = refs[:n_x], refs[n_x:n_x + n_w]
    hidden_ref, grads_ref, x_ref, w_ref, acc, x_sems, w_sems = refs[n_x + n_w + 3:]
    first = w_ref.shape[0] - n_w
    copies = load(x_parts, x_ref, x_sems, EARLY_CHUNKS) + load(w_parts, w_ref, w_sems, first)
    for copy in copies:
        copy.wait()

    def tile_step(tile, carry):
        @pl.when((tile >= first) | (pick[tile] >= EARLY_CHUNKS))
        def _():
            add_tile(tile, pick, names, x_ref, w_ref, acc)

        return carry

    lax.fori_loop(0, w_ref.shape[0], tile_step, 0)
    for j in range(grads_ref.shape[0]):
        columns = slice(j * SIDE, (j + 1) * SIDE)
        gate = acc[j, :, :SIDE]
        up = acc[j, :, SIDE:]
        sig = 1.0 / (1.0 + jnp.exp(-gate))
        silu = gate * sig
        hidden_ref[:, columns] = (silu * up).astype(jnp.bfloat16)
        upstream = up_ref[:, columns].astype(jnp.float32)
        grads_ref[j, :, :SIDE] = (
            upstream * up * sig * (1.0 + gate * (1.0 - sig))
        ).astype(jnp.bfloat16)
        grads_ref[j, :, SIDE:] = (upstream * silu).astype(jnp.bfloat16)


def cost(tiles, slots, tokens, read, exps):
    return pl.CostEstimate(
        flops=2 * tiles * slots * tokens * SIDE * 2 * SIDE,
        bytes_accessed=read,
        transcendentals=exps,
    )


def forward_early(pick, names, x_parts, w_parts, col_count):
    tokens, span = x_parts[0].shape[1:]
    depth, pair = w_parts[0].shape
    return pl.pallas_call(
        functools.partial(early_kernel, len(x_parts), len(w_parts)),
        in_specs=[SCALARS] * 2 + [ANYWHERE] * (len(x_parts) + len(w_parts)),
        out_specs=[ON_CHIP] * 3,
        out_shape=[
            pltpu.VMEM((16, tokens, span), jnp.bfloat16),
            pltpu.VMEM((16, depth, pair), jnp.bfloat16),
            pltpu.VMEM((col_count + 1, tokens, pair), jnp.float32),
        ],
        scratch_shapes=[
            pltpu.SemaphoreType.DMA((len(x_parts),)),
            pltpu.SemaphoreType.DMA((len(w_parts),)),
        ],
        compiler_params=pltpu.CompilerParams(vmem_limit_bytes=VMEM_LIMIT),
        cost_estimate=pl.CostEstimate(flops=0, bytes_accessed=0, transcendentals=0),
        name="forward_early",
    )(pick, names, *x_parts, *w_parts)


def forward_late(pick, names, upstream, x_parts, w_parts, x, w, acc):
    tokens, width = upstream.shape
    col_count = width // SIDE
    parts = len(x_parts) + len(w_parts)
    hidden, grads, _, w, _ = pl.pallas_call(
        functools.partial(late_kernel, len(x_parts), len(w_parts)),
        in_specs=[SCALARS] * 2 + [ON_CHIP] + [ANYWHERE] * parts + [ON_CHIP] * 3,
        out_specs=[ON_CHIP] * 5,
        out_shape=[
            jax.ShapeDtypeStruct((tokens, width), jnp.bfloat16),
            pltpu.VMEM((col_count, tokens, 2 * SIDE), jnp.bfloat16),
        ] + [pltpu.VMEM(kept.shape, kept.dtype) for kept in (x, w, acc)],
        input_output_aliases={3 + parts: 2, 4 + parts: 3, 5 + parts: 4},
        scratch_shapes=[
            pltpu.SemaphoreType.DMA((len(x_parts),)),
            pltpu.SemaphoreType.DMA((len(w_parts),)),
        ],
        compiler_params=pltpu.CompilerParams(vmem_limit_bytes=VMEM_LIMIT),
        cost_estimate=cost(len(w_parts) + 2, names.shape[1] // 2, tokens, 10 * upstream.size, 2 * upstream.size),
        name="forward_late",
    )(pick, names, upstream, *x_parts, *w_parts, x, w, acc)
    return hidden, grads, w


def backward_kernel(jobs, places, names, grads_ref, w_ref, *refs):
    slots = names.shape[1] // 2
    col_count = grads_ref.shape[0]
    outs = [k for k, _, _ in jobs]
    n_out = max(outs) + 1
    acc = refs[-1]
    added, outs = refs[:-1 - n_out], refs[-1 - n_out:-1]
    filled = [0] * n_out
    for k, position, sources in jobs:
        for j in range(3):
            columns = slice(j * SIDE, (j + 1) * SIDE)
            start = jnp.zeros(acc.shape[1:], jnp.float32)
            for number, part in sources:
                start += added[number][part, :, columns].astype(jnp.float32)
            acc[j] = start
        tile = places[position]
        for slot in range(slots):
            row = names[tile, slot]
            col = jnp.minimum(names[tile, slots + slot], col_count - 1)
            acc[row] += lax.dot_general(
                grads_ref[col],
                slot_of(w_ref, tile, slot),
                (((1,), (1,)), ((), ())),
                preferred_element_type=jnp.float32,
            )
        for j in range(3):
            outs[k][filled[k], :, j * SIDE:(j + 1) * SIDE] = acc[j].astype(outs[k].dtype)
        filled[k] += 1


def backward(jobs, added, places, names, grads, w):
    tokens = grads.shape[1]
    n_out = max(k for k, _, _ in jobs) + 1
    sizes = [sum(k == out for k, _, _ in jobs) for out in range(n_out)]
    return pl.pallas_call(
        functools.partial(backward_kernel, jobs),
        in_specs=[SCALARS] * 2 + [ON_CHIP] * (2 + len(added)),
        out_specs=[ON_CHIP] * n_out,
        out_shape=[jax.ShapeDtypeStruct((size, tokens, 3 * SIDE), jnp.bfloat16) for size in sizes],
        scratch_shapes=[pltpu.VMEM((4, tokens, SIDE), jnp.float32)],
        compiler_params=pltpu.CompilerParams(vmem_limit_bytes=VMEM_LIMIT),
        cost_estimate=cost(len(jobs), names.shape[1] // 2, tokens, 2 * len(jobs) * w.size // w.shape[0], 0),
        name="backward",
    )(places, names, grads, w, *added)


def after(value, *others):
    return lax.optimization_barrier((value,) + others)[0]


def gather(own, tokens):
    def swap(value):
        return shift(value, "core", 1)

    barrier = lax.optimization_barrier
    across = shift(tokens, "x_hi", 1)
    a1, t0 = turn(own, 1), swap(own)
    b1 = shift(after(own, t0), "x_lo", 1)
    a1, across = barrier((a1, across))
    both = jnp.stack([tokens, across])
    a2 = turn(a1, 1)
    p1, m1 = shift(both, "z", 1), shift(both, "z", -1)
    t1 = swap(a1)
    a2, p1, m1, b1, t1 = barrier((a2, p1, m1, b1, t1))
    c1, a3, b2 = turn(b1, -1), turn(a2, 1), shift(a1, "x_lo", 1)
    p2, m2 = shift(p1, "z", 1), shift(m1, "z", -1)
    c1, a3, b2, p2, m2, b1, a2 = barrier((c1, a3, b2, p2, m2, b1, a2))
    c2 = turn(c1, -1)
    p3, m3 = shift(p2, "z", 1), shift(m2, "z", -1)
    p4, m4 = shift(p3[0], "z", 1), shift(m3[1], "z", -1)
    return (own, t0, a1, t1, b1, a2, c1, a3, b2), c2, (both, p1, m1, p2, m2), (p3, m3, p4, m4)


def on_device(tokens, gate_blocks, up_blocks, block_row, block_col, upstream):
    table = lax.dynamic_slice_in_dim(jnp.asarray(PLANS), lax.axis_index(AXES), 1)[0]
    tokens, gate_blocks, table = lax.optimization_barrier((tokens, gate_blocks, table))
    pick, places = table[:16], table[16:]
    slots = gate_blocks.shape[0]
    i32, bf16 = jnp.int32, jnp.bfloat16
    ids = jnp.concatenate([
        jnp.where(block_row < 0, 3, block_row % 3),
        jnp.where(block_row < 0, 12, block_col % 12),
    ]).astype(bf16)
    ids = jnp.broadcast_to(jnp.pad(ids, (0, 2 * SIDE - 2 * slots))[None], (16, 2 * SIDE))
    blocks = jnp.concatenate([gate_blocks, up_blocks], axis=2).reshape(slots * SIDE, 2 * SIDE)
    w_early, c2, x_early, x_late = gather(jnp.concatenate([blocks, ids]), tokens)

    line = lax.broadcasted_iota(i32, (16, 2 * slots), 0)

    def names_of(parts):
        names = jnp.zeros((16, 2 * slots), jnp.float32)
        for place, part in enumerate(parts):
            name = part[slots * SIDE:slots * SIDE + 1, :2 * slots].astype(jnp.float32)
            names = jnp.where(line == place, name, names)
        return names.astype(i32)

    x, w, acc = forward_early(pick, names_of(w_early), x_early, w_early, upstream.shape[1] // SIDE)
    moved, acc = lax.optimization_barrier((w_early[4:], acc))
    w_late = [shift(part, "core", 1) for part in moved] + [c2, shift(c2, "core", 1)]
    names = names_of(w_early + tuple(w_late))
    hidden, grads, w = forward_late(pick, names, upstream, x_late, w_late, x, w, acc)

    def share(jobs, added):
        return backward(jobs, added, places, names, grads, w)

    x4, x3 = share([(0, 0, ()), (1, 1, ()), (1, 2, ())], [])
    x4, x3 = shift(x4, "x_hi", 1), shift(x3, "x_hi", 1)
    plus, x2 = share([(0, 8, ((0, 0),)), (1, 3, ()), (1, 4, ())], [x4])
    plus, x2 = shift(plus, "z", 1), shift(x2, "x_hi", 1)
    plus, minus, x1 = share(
        [(0, 9, ((0, 0), (1, 0))), (1, 10, ((0, 1),)), (2, 5, ()), (2, 6, ())], [x3, plus])
    plus, minus, x1 = shift(plus, "z", 1), shift(minus, "z", -1), shift(x1, "x_hi", 1)
    plus, minus, x0 = share(
        [(0, 11, ((0, 0), (1, 0))), (1, 12, ((0, 1), (2, 0))), (2, 7, ())], [x2, plus, minus])
    plus, minus, x0 = shift(plus, "z", 1), shift(minus, "z", -1), shift(x0, "x_hi", 1)
    plus, minus = share(
        [(0, 13, ((0, 0), (1, 0))), (1, 14, ((0, 1), (2, 0)))], [x1, plus, minus])
    plus, minus = shift(plus, "z", 1), shift(minus, "z", -1)
    grad_tokens, = share([(0, 15, ((0, 0), (1, 0), (2, 0)))], [x0, plus, minus])
    return hidden, grad_tokens[0]


def solution(mesh):
    fine = Mesh(mesh.devices.reshape([SIZES[a] for a in AXES]), AXES)
    both = P(ROW, COL)
    return jax.shard_map(
        on_device,
        mesh=fine,
        in_specs=(both, P(ROW + COL, None, None), P(ROW + COL, None, None), P(ROW + COL), P(ROW + COL), both),
        out_specs=(both, both),
        check_vma=False,
    )
```

```python
import functools

import jax
import jax.numpy as jnp
import numpy as np
from jax import lax
from jax.experimental import pallas as pl
from jax.experimental.pallas import tpu as pltpu
from jax.sharding import Mesh, PartitionSpec as P

AXES = ("y", "x_lo", "core", "x_hi", "z")
ROW = ("y", "x_lo", "core")
COL = ("x_hi", "z")
SIZES = {"y": 4, "x_lo": 2, "core": 2, "x_hi": 2, "z": 8}
SIDE = 128
EARLY_CHUNKS = 14
ORDER = (4, 3, -3, 2, -2, 1, -1, 0)
VMEM_LIMIT = 10 * 1024 * 1024
ON_CHIP = pl.BlockSpec(memory_space=pltpu.VMEM)
ANYWHERE = pl.BlockSpec(memory_space=pl.ANY)
SCALARS = pl.BlockSpec(memory_space=pltpu.SMEM)


TILES = [
    (0, 0, 0), (0, 0, 1), (-1, 0, 0), (-1, 0, 1), (0, 1, 0), (-2, 0, 0),
    (1, 1, 0), (-3, 0, 0), (-1, 1, 0),
    (0, 1, 1), (-2, 0, 1), (1, 1, 1), (-3, 0, 1), (-1, 1, 1),
    (2, 1, 0), (2, 1, 1),
]
CHUNKS = [(hi, dz) for dz in (0, -1, 1, -2, 2, -3, 3, 4) for hi in (0, 1)]


def plans():
    table = []
    for y, x_lo, core, x_hi, z in np.ndindex(*(SIZES[a] for a in AXES)):
        tiles = []
        for step, other_x, other_core in TILES:
            c = (core + other_core) % 2
            tiles.append((y + step * (1 - 2 * c)) % 4 * 4 + (x_lo + other_x) % 2 * 2 + c)
        chunks = [(x_hi + other) % 2 * 8 + (z + dz) % 8 for other, dz in CHUNKS]
        columns = [(x_hi + other) % 2 * 8 + (z + dz) % 8 for other in (1, 0) for dz in ORDER]
        table.append([chunks.index(k) for k in tiles] + [tiles.index(k) for k in columns])
    return np.array(table, np.int32)


PLANS = plans()


def shift(value, axis, step):
    size = SIZES[axis]
    return lax.ppermute(value, axis, [(i, (i + step) % size) for i in range(size)])


def turn(value, sign):
    pairs = []
    for y in range(4):
        for core, step in ((0, sign), (1, -sign)):
            pairs.append((y * 2 + core, (y + step) % 4 * 2 + core))
    return lax.ppermute(value, ("y", "core"), pairs)


def slot_of(ref, tile, slot):
    return ref[tile, slot * SIDE:(slot + 1) * SIDE]


def load(parts, whole, sems, first):
    copies = []
    for number, part in enumerate(parts):
        if len(part.shape) == len(whole.shape):
            place, first = whole.at[pl.ds(first, part.shape[0])], first + part.shape[0]
        else:
            place, first = whole.at[first], first + 1
        copy = pltpu.make_async_copy(part, place, sems.at[number])
        copy.start()
        copies.append(copy)
    return copies


def store_kernel(n_x, n_w, first_x, first_w, *refs):
    x_parts, w_parts = refs[:n_x], refs[n_x:n_x + n_w]
    x_ref, w_ref, x_sems, w_sems = refs[-4:]
    copies = load(x_parts, x_ref, x_sems, first_x) + load(w_parts, w_ref, w_sems, first_w)
    for copy in copies:
        copy.wait()


def store(x_parts, w_parts, first_x, first_w, kept=()):
    parts = len(x_parts) + len(w_parts)
    return pl.pallas_call(
        functools.partial(store_kernel, len(x_parts), len(w_parts), first_x, first_w),
        in_specs=[ANYWHERE] * parts + [ON_CHIP] * len(kept),
        out_specs=[ON_CHIP] * 2,
        out_shape=[
            pltpu.VMEM((len(CHUNKS),) + x_parts[0].shape[1:], jnp.bfloat16),
            pltpu.VMEM((len(TILES),) + w_parts[0].shape, jnp.bfloat16),
        ],
        input_output_aliases={parts + number: number for number in range(len(kept))},
        scratch_shapes=[
            pltpu.SemaphoreType.DMA((len(x_parts),)),
            pltpu.SemaphoreType.DMA((len(w_parts),)),
        ],
        compiler_params=pltpu.CompilerParams(vmem_limit_bytes=VMEM_LIMIT),
        cost_estimate=pl.CostEstimate(flops=0, bytes_accessed=4 * parts * w_parts[0].size, transcendentals=0),
        name="store",
    )(*x_parts, *w_parts, *kept)


def add_tile(tile, pick, names, x_ref, w_ref, acc):
    slots = names.shape[1] // 2
    for slot in range(slots):
        row = jnp.minimum(names[tile, slot], 2)
        col = names[tile, slots + slot]
        taken = x_ref[pick[tile], :, pl.ds(pl.multiple_of(row * SIDE, SIDE), SIDE)]
        acc[col] += jnp.dot(taken, slot_of(w_ref, tile, slot), preferred_element_type=jnp.float32)


def early_kernel(n_x, n_w, first_x, first_w, pick, names, *refs):
    x_parts, w_parts = refs[:n_x], refs[n_x:n_x + n_w]
    x_ref, w_ref, acc, x_sems, w_sems = refs[n_x + n_w + 2:]
    copies = load(x_parts, x_ref, x_sems, first_x) + load(w_parts, w_ref, w_sems, first_w)
    acc[...] = jnp.zeros_like(acc)
    for copy in copies:
        copy.wait()

    def tile_step(tile, carry):
        @pl.when(pick[tile] < EARLY_CHUNKS)
        def _():
            add_tile(tile, pick, names, x_ref, w_ref, acc)

        return carry

    lax.fori_loop(0, first_w + n_w, tile_step, 0)


def late_kernel(n_x, n_w, pick, names, up_ref, *refs):
    x_parts, w_parts = refs[:n_x], refs[n_x:n_x + n_w]
    hidden_ref, grads_ref, x_ref, w_ref, acc, x_sems, w_sems = refs[n_x + n_w + 3:]
    first = w_ref.shape[0] - n_w
    copies = load(x_parts, x_ref, x_sems, EARLY_CHUNKS) + load(w_parts, w_ref, w_sems, first)
    for copy in copies:
        copy.wait()

    def tile_step(tile, carry):
        @pl.when((tile >= first) | (pick[tile] >= EARLY_CHUNKS))
        def _():
            add_tile(tile, pick, names, x_ref, w_ref, acc)

        return carry

    lax.fori_loop(0, w_ref.shape[0], tile_step, 0)
    for j in range(grads_ref.shape[0]):
        columns = slice(j * SIDE, (j + 1) * SIDE)
        gate = acc[j, :, :SIDE]
        up = acc[j, :, SIDE:]
        sig = 1.0 / (1.0 + jnp.exp(-gate))
        silu = gate * sig
        hidden_ref[:, columns] = (silu * up).astype(jnp.bfloat16)
        upstream = up_ref[:, columns].astype(jnp.float32)
        grads_ref[j, :, :SIDE] = (
            upstream * up * sig * (1.0 + gate * (1.0 - sig))
        ).astype(jnp.bfloat16)
        grads_ref[j, :, SIDE:] = (upstream * silu).astype(jnp.bfloat16)


def cost(tiles, slots, tokens, read, exps):
    return pl.CostEstimate(
        flops=2 * tiles * slots * tokens * SIDE * 2 * SIDE,
        bytes_accessed=read,
        transcendentals=exps,
    )


def forward_early(pick, names, x_parts, w_parts, x, w, col_count):
    tokens = x.shape[1]
    depth, pair = w_parts[0].shape
    parts = len(x_parts) + len(w_parts)
    first_w = len(TILES) - 2 - len(w_parts)
    first_x = EARLY_CHUNKS - 2 * len(x_parts)
    return pl.pallas_call(
        functools.partial(early_kernel, len(x_parts), len(w_parts), first_x, first_w),
        in_specs=[SCALARS] * 2 + [ANYWHERE] * parts + [ON_CHIP] * 2,
        out_specs=[ON_CHIP] * 3,
        out_shape=[pltpu.VMEM(kept.shape, kept.dtype) for kept in (x, w)] + [
            pltpu.VMEM((col_count + 1, tokens, pair), jnp.float32),
        ],
        input_output_aliases={2 + parts: 0, 3 + parts: 1},
        scratch_shapes=[
            pltpu.SemaphoreType.DMA((len(x_parts),)),
            pltpu.SemaphoreType.DMA((len(w_parts),)),
        ],
        compiler_params=pltpu.CompilerParams(vmem_limit_bytes=VMEM_LIMIT),
        cost_estimate=pl.CostEstimate(flops=0, bytes_accessed=0, transcendentals=0),
        name="forward_early",
    )(pick, names, *x_parts, *w_parts, x, w)


def forward_late(pick, names, upstream, x_parts, w_parts, x, w, acc):
    tokens, width = upstream.shape
    col_count = width // SIDE
    parts = len(x_parts) + len(w_parts)
    hidden, grads, _, w, _ = pl.pallas_call(
        functools.partial(late_kernel, len(x_parts), len(w_parts)),
        in_specs=[SCALARS] * 2 + [ON_CHIP] + [ANYWHERE] * parts + [ON_CHIP] * 3,
        out_specs=[ON_CHIP] * 5,
        out_shape=[
            jax.ShapeDtypeStruct((tokens, width), jnp.bfloat16),
            pltpu.VMEM((col_count, tokens, 2 * SIDE), jnp.bfloat16),
        ] + [pltpu.VMEM(kept.shape, kept.dtype) for kept in (x, w, acc)],
        input_output_aliases={3 + parts: 2, 4 + parts: 3, 5 + parts: 4},
        scratch_shapes=[
            pltpu.SemaphoreType.DMA((len(x_parts),)),
            pltpu.SemaphoreType.DMA((len(w_parts),)),
        ],
        compiler_params=pltpu.CompilerParams(vmem_limit_bytes=VMEM_LIMIT),
        cost_estimate=cost(len(w_parts) + 2, names.shape[1] // 2, tokens, 10 * upstream.size, 2 * upstream.size),
        name="forward_late",
    )(pick, names, upstream, *x_parts, *w_parts, x, w, acc)
    return hidden, grads, w


def backward_kernel(jobs, places, names, grads_ref, w_ref, *refs):
    slots = names.shape[1] // 2
    col_count = grads_ref.shape[0]
    outs = [k for k, _, _ in jobs]
    n_out = max(outs) + 1
    acc = refs[-1]
    added, outs = refs[:-1 - n_out], refs[-1 - n_out:-1]
    filled = [0] * n_out
    for k, position, sources in jobs:
        for j in range(3):
            columns = slice(j * SIDE, (j + 1) * SIDE)
            start = jnp.zeros(acc.shape[1:], jnp.float32)
            for number, part in sources:
                start += added[number][part, :, columns].astype(jnp.float32)
            acc[j] = start
        tile = places[position]
        for slot in range(slots):
            row = names[tile, slot]
            col = jnp.minimum(names[tile, slots + slot], col_count - 1)
            acc[row] += lax.dot_general(
                grads_ref[col],
                slot_of(w_ref, tile, slot),
                (((1,), (1,)), ((), ())),
                preferred_element_type=jnp.float32,
            )
        for j in range(3):
            outs[k][filled[k], :, j * SIDE:(j + 1) * SIDE] = acc[j].astype(outs[k].dtype)
        filled[k] += 1


def backward(jobs, added, places, names, grads, w):
    tokens = grads.shape[1]
    n_out = max(k for k, _, _ in jobs) + 1
    sizes = [sum(k == out for k, _, _ in jobs) for out in range(n_out)]
    return pl.pallas_call(
        functools.partial(backward_kernel, jobs),
        in_specs=[SCALARS] * 2 + [ON_CHIP] * (2 + len(added)),
        out_specs=[ON_CHIP] * n_out,
        out_shape=[jax.ShapeDtypeStruct((size, tokens, 3 * SIDE), jnp.bfloat16) for size in sizes],
        scratch_shapes=[pltpu.VMEM((4, tokens, SIDE), jnp.float32)],
        compiler_params=pltpu.CompilerParams(vmem_limit_bytes=VMEM_LIMIT),
        cost_estimate=cost(len(jobs), names.shape[1] // 2, tokens, 2 * len(jobs) * w.size // w.shape[0], 0),
        name="backward",
    )(places, names, grads, w, *added)


def after(value, *others):
    return lax.optimization_barrier((value,) + others)[0]


def gather(own, tokens):
    def swap(value):
        return shift(value, "core", 1)

    barrier = lax.optimization_barrier
    across = shift(tokens, "x_hi", 1)
    a1, t0 = turn(own, 1), swap(own)
    b1 = shift(after(own, t0), "x_lo", 1)
    a1, across = barrier((a1, across))
    both = jnp.stack([tokens, across])
    a2 = turn(a1, 1)
    p1, m1 = shift(both, "z", 1), shift(both, "z", -1)
    t1 = swap(a1)
    a2, p1, m1, b1, t1 = barrier((a2, p1, m1, b1, t1))
    c1, a3, b2 = turn(b1, -1), turn(a2, 1), shift(a1, "x_lo", 1)
    kept = store((both, p1, m1), (own, t0, a1, t1, b1, a2), 0, 0)
    p2, m2 = shift(p1, "z", 1), shift(m1, "z", -1)
    p2, m2, kept = barrier((p2, m2, kept))
    p3, m3 = shift(p2, "z", 1), shift(m2, "z", -1)
    x, w = store((p2, m2), (c1, a3, b2), 6, 6, kept)
    c2 = turn(c1, -1)
    t2, t3 = swap(b1), swap(a2)
    p3, m3, c1, a3, b2, t2, t3 = barrier((p3, m3, c1, a3, b2, t2, t3))
    t5, t6, t4 = swap(c1), swap(a3), swap(b2)
    p4, m4 = shift(p3[0], "z", 1), shift(m3[1], "z", -1)
    known = (own, t0, a1, t1, b1, a2, c1, a3, b2, t2, t3, t5, t6, t4)
    return x, w, (p3, m3), (t2, t3, t5, t6, t4), (p4, m4), c2, known


def on_device(tokens, gate_blocks, up_blocks, block_row, block_col, upstream):
    table = lax.dynamic_slice_in_dim(jnp.asarray(PLANS), lax.axis_index(AXES), 1)[0]
    tokens, gate_blocks, table = lax.optimization_barrier((tokens, gate_blocks, table))
    pick, places = table[:16], table[16:]
    slots = gate_blocks.shape[0]
    i32, bf16 = jnp.int32, jnp.bfloat16
    ids = jnp.concatenate([
        jnp.where(block_row < 0, 3, block_row % 3),
        jnp.where(block_row < 0, 12, block_col % 12),
    ]).astype(bf16)
    ids = jnp.broadcast_to(jnp.pad(ids, (0, 2 * SIDE - 2 * slots))[None], (16, 2 * SIDE))
    blocks = jnp.concatenate([gate_blocks, up_blocks], axis=2).reshape(slots * SIDE, 2 * SIDE)
    x, w, x_early, w_early, x_late, c2, known = gather(jnp.concatenate([blocks, ids]), tokens)

    line = lax.broadcasted_iota(i32, (16, 2 * slots), 0)

    def names_of(parts):
        names = jnp.zeros((16, 2 * slots), jnp.float32)
        for place, part in enumerate(parts):
            name = part[slots * SIDE:slots * SIDE + 1, :2 * slots].astype(jnp.float32)
            names = jnp.where(line == place, name, names)
        return names.astype(i32)

    x, w, acc = forward_early(pick, names_of(known), x_early, w_early, x, w, upstream.shape[1] // SIDE)
    c2, acc, x_late = lax.optimization_barrier((c2, acc, x_late))
    w_late = (c2, shift(c2, "core", 1))
    names = names_of(known + w_late)
    hidden, grads, w = forward_late(pick, names, upstream, x_late, w_late, x, w, acc)

    def share(jobs, added):
        return backward(jobs, added, places, names, grads, w)

    x4, x3 = share([(0, 0, ()), (1, 1, ()), (1, 2, ())], [])
    x4, x3 = shift(x4, "x_hi", 1), shift(x3, "x_hi", 1)
    plus, x2 = share([(0, 8, ((0, 0),)), (1, 3, ()), (1, 4, ())], [x4])
    plus, x2 = shift(plus, "z", 1), shift(x2, "x_hi", 1)
    plus, minus, x1 = share(
        [(0, 9, ((0, 0), (1, 0))), (1, 10, ((0, 1),)), (2, 5, ()), (2, 6, ())], [x3, plus])
    plus, minus, x1 = shift(plus, "z", 1), shift(minus, "z", -1), shift(x1, "x_hi", 1)
    plus, minus, x0 = share(
        [(0, 11, ((0, 0), (1, 0))), (1, 12, ((0, 1), (2, 0))), (2, 7, ())], [x2, plus, minus])
    plus, minus, x0 = shift(plus, "z", 1), shift(minus, "z", -1), shift(x0, "x_hi", 1)
    plus, minus = share(
        [(0, 13, ((0, 0), (1, 0))), (1, 14, ((0, 1), (2, 0)))], [x1, plus, minus])
    plus, minus = shift(plus, "z", 1), shift(minus, "z", -1)
    grad_tokens, = share([(0, 15, ((0, 0), (1, 0), (2, 0)))], [x0, plus, minus])
    return hidden, grad_tokens[0]


def solution(mesh):
    fine = Mesh(mesh.devices.reshape([SIZES[a] for a in AXES]), AXES)
    both = P(ROW, COL)
    return jax.shard_map(
        on_device,
        mesh=fine,
        in_specs=(both, P(ROW + COL, None, None), P(ROW + COL, None, None), P(ROW + COL), P(ROW + COL), both),
        out_specs=(both, both),
        check_vma=False,
    )
```

```python
import functools

import jax
import jax.numpy as jnp
import numpy as np
from jax import lax
from jax.experimental import pallas as pl
from jax.experimental.pallas import tpu as pltpu
from jax.sharding import Mesh, PartitionSpec as P

AXES = ("y", "x_lo", "core", "x_hi", "z")
ROW = ("y", "x_lo", "core")
COL = ("x_hi", "z")
SIZES = {"y": 4, "x_lo": 2, "core": 2, "x_hi": 2, "z": 8}
SIDE = 128
READY = ((9, 10), (14, 14), (16, 16))
ORDER = (4, 3, -3, 2, -2, 1, -1, 0)
VMEM_LIMIT = 10 * 1024 * 1024
ON_CHIP = pl.BlockSpec(memory_space=pltpu.VMEM)
ANYWHERE = pl.BlockSpec(memory_space=pl.ANY)
SCALARS = pl.BlockSpec(memory_space=pltpu.SMEM)


TILES = [
    (0, 0, 0), (0, 0, 1), (-1, 0, 0), (-1, 0, 1), (0, 1, 0), (-2, 0, 0),
    (1, 1, 0), (-3, 0, 0), (-1, 1, 0),
    (0, 1, 1), (-2, 0, 1), (1, 1, 1), (-3, 0, 1), (-1, 1, 1),
    (2, 1, 0), (2, 1, 1),
]
CHUNKS = [(hi, dz) for dz in (0, -1, 1, -2, 2, -3, 3, 4) for hi in (0, 1)]


def plans():
    table = []
    for y, x_lo, core, x_hi, z in np.ndindex(*(SIZES[a] for a in AXES)):
        tiles = []
        for step, other_x, other_core in TILES:
            c = (core + other_core) % 2
            tiles.append((y + step * (1 - 2 * c)) % 4 * 4 + (x_lo + other_x) % 2 * 2 + c)
        chunks = [(x_hi + other) % 2 * 8 + (z + dz) % 8 for other, dz in CHUNKS]
        columns = [(x_hi + other) % 2 * 8 + (z + dz) % 8 for other in (1, 0) for dz in ORDER]
        table.append([chunks.index(k) for k in tiles] + [tiles.index(k) for k in columns])
    return np.array(table, np.int32)


PLANS = plans()


def shift(value, axis, step):
    size = SIZES[axis]
    return lax.ppermute(value, axis, [(i, (i + step) % size) for i in range(size)])


def turn(value, sign):
    pairs = []
    for y in range(4):
        for core, step in ((0, sign), (1, -sign)):
            pairs.append((y * 2 + core, (y + step) % 4 * 2 + core))
    return lax.ppermute(value, ("y", "core"), pairs)


def slot_of(ref, tile, slot):
    return ref[tile, slot * SIDE:(slot + 1) * SIDE]


def load(parts, whole, sems, first):
    copies = []
    for number, part in enumerate(parts):
        if len(part.shape) == len(whole.shape):
            place, first = whole.at[pl.ds(first, part.shape[0])], first + part.shape[0]
        else:
            place, first = whole.at[first], first + 1
        copy = pltpu.make_async_copy(part, place, sems.at[number])
        copy.start()
        copies.append(copy)
    return copies


def store_kernel(n_x, n_w, first_x, first_w, *refs):
    x_parts, w_parts = refs[:n_x], refs[n_x:n_x + n_w]
    x_ref, w_ref, x_sems, w_sems = refs[-4:]
    copies = load(x_parts, x_ref, x_sems, first_x) + load(w_parts, w_ref, w_sems, first_w)
    for copy in copies:
        copy.wait()


def store(x_parts, w_parts, first_x, first_w, kept=()):
    parts = len(x_parts) + len(w_parts)
    return pl.pallas_call(
        functools.partial(store_kernel, len(x_parts), len(w_parts), first_x, first_w),
        in_specs=[ANYWHERE] * parts + [ON_CHIP] * len(kept),
        out_specs=[ON_CHIP] * 2,
        out_shape=[
            pltpu.VMEM((len(CHUNKS),) + x_parts[0].shape[1:], jnp.bfloat16),
            pltpu.VMEM((len(TILES),) + w_parts[0].shape, jnp.bfloat16),
        ],
        input_output_aliases={parts + number: number for number in range(len(kept))},
        scratch_shapes=[
            pltpu.SemaphoreType.DMA((len(x_parts),)),
            pltpu.SemaphoreType.DMA((len(w_parts),)),
        ],
        compiler_params=pltpu.CompilerParams(vmem_limit_bytes=VMEM_LIMIT),
        cost_estimate=pl.CostEstimate(flops=0, bytes_accessed=4 * parts * w_parts[0].size, transcendentals=0),
        name="store",
    )(*x_parts, *w_parts, *kept)


def add_tile(tile, pick, names, x_ref, w_ref, acc):
    slots = names.shape[1] // 2
    for slot in range(slots):
        row = jnp.minimum(names[tile, slot], 2)
        col = names[tile, slots + slot]
        taken = x_ref[pick[tile], :, pl.ds(pl.multiple_of(row * SIDE, SIDE), SIDE)]
        acc[col] += jnp.dot(taken, slot_of(w_ref, tile, slot), preferred_element_type=jnp.float32)


def ready(tile, pick, stage):
    tiles, chunks = READY[stage]
    return (tile < tiles) & (pick[tile] < chunks)


def add_stage(stage, x_parts, w_parts, pick, names, x_ref, w_ref, acc, x_sems, w_sems):
    tiles, chunks = READY[stage]
    count = sum(part.shape[0] if len(part.shape) == 3 else 1 for part in x_parts)
    copies = load(x_parts, x_ref, x_sems, chunks - count)
    copies += load(w_parts, w_ref, w_sems, tiles - len(w_parts))
    if stage == 0:
        acc[...] = jnp.zeros_like(acc)
    for copy in copies:
        copy.wait()

    def tile_step(tile, carry):
        new = ready(tile, pick, stage)
        if stage > 0:
            new = new & jnp.logical_not(ready(tile, pick, stage - 1))

        @pl.when(new)
        def _():
            add_tile(tile, pick, names, x_ref, w_ref, acc)

        return carry

    lax.fori_loop(0, tiles, tile_step, 0)


def early_kernel(stage, n_x, n_w, n_kept, pick, names, *refs):
    add_stage(stage, refs[:n_x], refs[n_x:n_x + n_w], pick, names, *refs[n_x + n_w + n_kept:])


def late_kernel(n_x, n_w, pick, names, up_ref, *refs):
    hidden_ref, grads_ref, *rest = refs[n_x + n_w + 3:]
    acc = rest[2]
    add_stage(2, refs[:n_x], refs[n_x:n_x + n_w], pick, names, *rest)
    for j in range(grads_ref.shape[0]):
        columns = slice(j * SIDE, (j + 1) * SIDE)
        gate = acc[j, :, :SIDE]
        up = acc[j, :, SIDE:]
        sig = 1.0 / (1.0 + jnp.exp(-gate))
        silu = gate * sig
        hidden_ref[:, columns] = (silu * up).astype(jnp.bfloat16)
        upstream = up_ref[:, columns].astype(jnp.float32)
        grads_ref[j, :, :SIDE] = (
            upstream * up * sig * (1.0 + gate * (1.0 - sig))
        ).astype(jnp.bfloat16)
        grads_ref[j, :, SIDE:] = (upstream * silu).astype(jnp.bfloat16)


def cost(tiles, slots, tokens, read, exps):
    return pl.CostEstimate(
        flops=2 * tiles * slots * tokens * SIDE * 2 * SIDE,
        bytes_accessed=read,
        transcendentals=exps,
    )


def forward_early(stage, pick, names, x_parts, w_parts, kept, col_count):
    tokens = kept[0].shape[1]
    parts = len(x_parts) + len(w_parts)
    return pl.pallas_call(
        functools.partial(early_kernel, stage, len(x_parts), len(w_parts), len(kept)),
        in_specs=[SCALARS] * 2 + [ANYWHERE] * parts + [ON_CHIP] * len(kept),
        out_specs=[ON_CHIP] * 3,
        out_shape=[pltpu.VMEM(array.shape, array.dtype) for array in kept[:2]] + [
            pltpu.VMEM((col_count + 1, tokens, 2 * SIDE), jnp.float32),
        ],
        input_output_aliases={2 + parts + number: number for number in range(len(kept))},
        scratch_shapes=[
            pltpu.SemaphoreType.DMA((len(x_parts),)),
            pltpu.SemaphoreType.DMA((len(w_parts),)),
        ],
        compiler_params=pltpu.CompilerParams(vmem_limit_bytes=VMEM_LIMIT),
        cost_estimate=cost(6 * (1 - stage), names.shape[1] // 2, tokens, 6 * (1 - stage) << 20, 0),
        name="forward_early",
    )(pick, names, *x_parts, *w_parts, *kept)


def forward_late(pick, names, upstream, x_parts, w_parts, x, w, acc):
    tokens, width = upstream.shape
    col_count = width // SIDE
    parts = len(x_parts) + len(w_parts)
    hidden, grads, _, w, _ = pl.pallas_call(
        functools.partial(late_kernel, len(x_parts), len(w_parts)),
        in_specs=[SCALARS] * 2 + [ON_CHIP] + [ANYWHERE] * parts + [ON_CHIP] * 3,
        out_specs=[ON_CHIP] * 5,
        out_shape=[
            jax.ShapeDtypeStruct((tokens, width), jnp.bfloat16),
            pltpu.VMEM((col_count, tokens, 2 * SIDE), jnp.bfloat16),
        ] + [pltpu.VMEM(kept.shape, kept.dtype) for kept in (x, w, acc)],
        input_output_aliases={3 + parts: 2, 4 + parts: 3, 5 + parts: 4},
        scratch_shapes=[
            pltpu.SemaphoreType.DMA((len(x_parts),)),
            pltpu.SemaphoreType.DMA((len(w_parts),)),
        ],
        compiler_params=pltpu.CompilerParams(vmem_limit_bytes=VMEM_LIMIT),
        cost_estimate=cost(len(w_parts) + 2, names.shape[1] // 2, tokens, 10 * upstream.size, 2 * upstream.size),
        name="forward_late",
    )(pick, names, upstream, *x_parts, *w_parts, x, w, acc)
    return hidden, grads, w


def backward_kernel(jobs, places, names, grads_ref, w_ref, *refs):
    slots = names.shape[1] // 2
    col_count = grads_ref.shape[0]
    outs = [k for k, _, _ in jobs]
    n_out = max(outs) + 1
    acc = refs[-1]
    added, outs = refs[:-1 - n_out], refs[-1 - n_out:-1]
    filled = [0] * n_out
    for k, position, sources in jobs:
        for j in range(3):
            columns = slice(j * SIDE, (j + 1) * SIDE)
            start = jnp.zeros(acc.shape[1:], jnp.float32)
            for number, part in sources:
                start += added[number][part, :, columns].astype(jnp.float32)
            acc[j] = start
        tile = places[position]
        for slot in range(slots):
            row = names[tile, slot]
            col = jnp.minimum(names[tile, slots + slot], col_count - 1)
            acc[row] += lax.dot_general(
                grads_ref[col],
                slot_of(w_ref, tile, slot),
                (((1,), (1,)), ((), ())),
                preferred_element_type=jnp.float32,
            )
        for j in range(3):
            outs[k][filled[k], :, j * SIDE:(j + 1) * SIDE] = acc[j].astype(outs[k].dtype)
        filled[k] += 1


def backward(jobs, added, places, names, grads, w):
    tokens = grads.shape[1]
    n_out = max(k for k, _, _ in jobs) + 1
    sizes = [sum(k == out for k, _, _ in jobs) for out in range(n_out)]
    return pl.pallas_call(
        functools.partial(backward_kernel, jobs),
        in_specs=[SCALARS] * 2 + [ON_CHIP] * (2 + len(added)),
        out_specs=[ON_CHIP] * n_out,
        out_shape=[jax.ShapeDtypeStruct((size, tokens, 3 * SIDE), jnp.bfloat16) for size in sizes],
        scratch_shapes=[pltpu.VMEM((4, tokens, SIDE), jnp.float32)],
        compiler_params=pltpu.CompilerParams(vmem_limit_bytes=VMEM_LIMIT),
        cost_estimate=cost(len(jobs), names.shape[1] // 2, tokens, 2 * len(jobs) * w.size // w.shape[0], 0),
        name="backward",
    )(places, names, grads, w, *added)


def after(value, *others):
    return lax.optimization_barrier((value,) + others)[0]


def gather(own, tokens, first):
    def swap(value):
        return shift(value, "core", 1)

    barrier = lax.optimization_barrier
    across = shift(tokens, "x_hi", 1)
    a1, t0 = turn(own, 1), swap(own)
    b1 = shift(after(own, t0), "x_lo", 1)
    a1, across, t0 = barrier((a1, across, t0))
    both = jnp.stack([tokens, across])
    a2 = turn(a1, 1)
    p1, m1 = shift(both, "z", 1), shift(both, "z", -1)
    t1 = swap(a1)
    a2, p1, m1, t1 = barrier((a2, p1, m1, t1))
    c1, a3, b2 = turn(b1, -1), turn(a2, 1), shift(a1, "x_lo", 1)
    kept = store((both, p1, m1), (own, t0, a1, t1, b1, a2), 0, 0)
    p2, m2 = shift(p1, "z", 1), shift(m1, "z", -1)
    p2, m2, kept = barrier((p2, m2, kept))
    p3, m3 = shift(p2, "z", 1), shift(m2, "z", -1)
    c2 = turn(c1, -1)
    b1, a2, p2, m2 = barrier((b1, a2, p2, m2))
    t2, t3 = swap(b1), swap(a2)
    known = (own, t0, a1, t1, b1, a2, c1, a3, b2)
    kept = first(kept, known, (p2, m2), (c1, a3, b2))
    p3, m3, c1, a3, b2, t2, t3, kept = barrier((p3, m3, c1, a3, b2, t2, t3, kept))
    t5, t6, t4 = swap(c1), swap(a3), swap(b2)
    p4, m4 = shift(p3[0], "z", 1), shift(m3[1], "z", -1)
    return kept, known, (p3, m3), (t2, t3, t5, t6, t4), (p4, m4), c2


def on_device(tokens, gate_blocks, up_blocks, block_row, block_col, upstream):
    table = lax.dynamic_slice_in_dim(jnp.asarray(PLANS), lax.axis_index(AXES), 1)[0]
    tokens, gate_blocks, table = lax.optimization_barrier((tokens, gate_blocks, table))
    pick, places = table[:16], table[16:]
    slots = gate_blocks.shape[0]
    i32, bf16 = jnp.int32, jnp.bfloat16
    ids = jnp.concatenate([
        jnp.where(block_row < 0, 3, block_row % 3),
        jnp.where(block_row < 0, 12, block_col % 12),
    ]).astype(bf16)
    ids = jnp.broadcast_to(jnp.pad(ids, (0, 2 * SIDE - 2 * slots))[None], (16, 2 * SIDE))
    blocks = jnp.concatenate([gate_blocks, up_blocks], axis=2).reshape(slots * SIDE, 2 * SIDE)
    line = lax.broadcasted_iota(i32, (16, 2 * slots), 0)

    def names_of(parts):
        names = jnp.zeros((16, 2 * slots), jnp.float32)
        for place, part in enumerate(parts):
            name = part[slots * SIDE:slots * SIDE + 1, :2 * slots].astype(jnp.float32)
            names = jnp.where(line == place, name, names)
        return names.astype(i32)

    col_count = upstream.shape[1] // SIDE

    def first(kept, known, x_parts, w_parts):
        return forward_early(0, pick, names_of(known), x_parts, w_parts, kept, col_count)

    kept, known, x_early, w_early, x_late, c2 = gather(jnp.concatenate([blocks, ids]), tokens, first)
    known += w_early
    x, w, acc = forward_early(1, pick, names_of(known), x_early, w_early, kept, col_count)
    c2, acc, x_late = lax.optimization_barrier((c2, acc, x_late))
    w_late = (c2, shift(c2, "core", 1))
    names = names_of(known + w_late)
    hidden, grads, w = forward_late(pick, names, upstream, x_late, w_late, x, w, acc)

    def share(jobs, added):
        return backward(jobs, added, places, names, grads, w)

    x4, x3 = share([(0, 0, ()), (1, 1, ()), (1, 2, ())], [])
    x4, x3 = shift(x4, "x_hi", 1), shift(x3, "x_hi", 1)
    plus, x2 = share([(0, 8, ((0, 0),)), (1, 3, ()), (1, 4, ())], [x4])
    plus, x2 = shift(plus, "z", 1), shift(x2, "x_hi", 1)
    plus, minus, x1 = share(
        [(0, 9, ((0, 0), (1, 0))), (1, 10, ((0, 1),)), (2, 5, ()), (2, 6, ())], [x3, plus])
    plus, minus, x1 = shift(plus, "z", 1), shift(minus, "z", -1), shift(x1, "x_hi", 1)
    plus, minus, x0 = share(
        [(0, 11, ((0, 0), (1, 0))), (1, 12, ((0, 1), (2, 0))), (2, 7, ())], [x2, plus, minus])
    plus, minus, x0 = shift(plus, "z", 1), shift(minus, "z", -1), shift(x0, "x_hi", 1)
    plus, minus = share(
        [(0, 13, ((0, 0), (1, 0))), (1, 14, ((0, 1), (2, 0)))], [x1, plus, minus])
    plus, minus = shift(plus, "z", 1), shift(minus, "z", -1)
    grad_tokens, = share([(0, 15, ((0, 0), (1, 0), (2, 0)))], [x0, plus, minus])
    return hidden, grad_tokens[0]


def solution(mesh):
    fine = Mesh(mesh.devices.reshape([SIZES[a] for a in AXES]), AXES)
    both = P(ROW, COL)
    return jax.shard_map(
        on_device,
        mesh=fine,
        in_specs=(both, P(ROW + COL, None, None), P(ROW + COL, None, None), P(ROW + COL), P(ROW + COL), both),
        out_specs=(both, both),
        check_vma=False,
    )
```

```python
import functools

import jax
import jax.numpy as jnp
import numpy as np
from jax import lax
from jax.experimental import pallas as pl
from jax.experimental.pallas import tpu as pltpu
from jax.sharding import Mesh, PartitionSpec as P

AXES = ("y", "x_lo", "core", "x_hi", "z")
ROW = ("y", "x_lo", "core")
COL = ("x_hi", "z")
SIZES = {"y": 4, "x_lo": 2, "core": 2, "x_hi": 2, "z": 8}
SIDE = 128
READY = ((9, 10), (14, 14), (16, 16))
ORDER = (4, 3, -3, 2, -2, 1, -1, 0)
VMEM_LIMIT = 10 * 1024 * 1024
ON_CHIP = pl.BlockSpec(memory_space=pltpu.VMEM)
ANYWHERE = pl.BlockSpec(memory_space=pl.ANY)
SCALARS = pl.BlockSpec(memory_space=pltpu.SMEM)


TILES = [
    (0, 0, 0), (0, 0, 1), (-1, 0, 0), (-1, 0, 1), (0, 1, 0), (-2, 0, 0),
    (1, 1, 0), (-3, 0, 0), (-1, 1, 0),
    (0, 1, 1), (-2, 0, 1), (1, 1, 1), (-3, 0, 1), (-1, 1, 1),
    (2, 1, 0), (2, 1, 1),
]
CHUNKS = [(hi, dz) for dz in (0, -1, 1, -2, 2, -3, 3, 4) for hi in (0, 1)]


def plans():
    table = []
    for y, x_lo, core, x_hi, z in np.ndindex(*(SIZES[a] for a in AXES)):
        tiles = []
        for step, other_x, other_core in TILES:
            c = (core + other_core) % 2
            tiles.append((y + step * (1 - 2 * c)) % 4 * 4 + (x_lo + other_x) % 2 * 2 + c)
        chunks = [(x_hi + other) % 2 * 8 + (z + dz) % 8 for other, dz in CHUNKS]
        columns = [(x_hi + other) % 2 * 8 + (z + dz) % 8 for other in (1, 0) for dz in ORDER]
        table.append([chunks.index(k) for k in tiles] + [tiles.index(k) for k in columns])
    return np.array(table, np.int32)


PLANS = plans()


def shift(value, axis, step):
    size = SIZES[axis]
    return lax.ppermute(value, axis, [(i, (i + step) % size) for i in range(size)])


def turn(value, sign):
    pairs = []
    for y in range(4):
        for core, step in ((0, sign), (1, -sign)):
            pairs.append((y * 2 + core, (y + step) % 4 * 2 + core))
    return lax.ppermute(value, ("y", "core"), pairs)


def slot_of(ref, tile, slot):
    return ref[tile, slot * SIDE:(slot + 1) * SIDE]


def load(parts, whole, sems, first):
    copies = []
    for number, part in enumerate(parts):
        if len(part.shape) == len(whole.shape):
            place, first = whole.at[pl.ds(first, part.shape[0])], first + part.shape[0]
        else:
            place, first = whole.at[first], first + 1
        copy = pltpu.make_async_copy(part, place, sems.at[number])
        copy.start()
        copies.append(copy)
    return copies


def store_kernel(n_x, n_w, first_x, first_w, *refs):
    x_parts, w_parts = refs[:n_x], refs[n_x:n_x + n_w]
    x_ref, w_ref, x_sems, w_sems = refs[-4:]
    copies = load(x_parts, x_ref, x_sems, first_x) + load(w_parts, w_ref, w_sems, first_w)
    for copy in copies:
        copy.wait()


def store(x_parts, w_parts, first_x, first_w, kept=()):
    parts = len(x_parts) + len(w_parts)
    return pl.pallas_call(
        functools.partial(store_kernel, len(x_parts), len(w_parts), first_x, first_w),
        in_specs=[ANYWHERE] * parts + [ON_CHIP] * len(kept),
        out_specs=[ON_CHIP] * 2,
        out_shape=[
            pltpu.VMEM((len(CHUNKS),) + x_parts[0].shape[1:], jnp.bfloat16),
            pltpu.VMEM((len(TILES),) + w_parts[0].shape, jnp.bfloat16),
        ],
        input_output_aliases={parts + number: number for number in range(len(kept))},
        scratch_shapes=[
            pltpu.SemaphoreType.DMA((len(x_parts),)),
            pltpu.SemaphoreType.DMA((len(w_parts),)),
        ],
        compiler_params=pltpu.CompilerParams(vmem_limit_bytes=VMEM_LIMIT),
        cost_estimate=pl.CostEstimate(flops=0, bytes_accessed=4 * parts * w_parts[0].size, transcendentals=0),
        name="store",
    )(*x_parts, *w_parts, *kept)


def add_tile(tile, pick, names, x_ref, w_ref, acc):
    slots = names.shape[1] // 2
    for slot in range(slots):
        row = jnp.minimum(names[tile, slot], 2)
        col = names[tile, slots + slot]
        taken = x_ref[pick[tile], :, pl.ds(pl.multiple_of(row * SIDE, SIDE), SIDE)]
        acc[col] += jnp.dot(taken, slot_of(w_ref, tile, slot), preferred_element_type=jnp.float32)


def ready(tile, pick, stage):
    tiles, chunks = READY[stage]
    return (tile < tiles) & (pick[tile] < chunks)


def add_stage(stage, x_parts, w_parts, pick, names, x_ref, w_ref, acc, x_sems, w_sems):
    tiles, chunks = READY[stage]
    count = sum(part.shape[0] if len(part.shape) == 3 else 1 for part in x_parts)
    copies = load(x_parts, x_ref, x_sems, chunks - count)
    copies += load(w_parts, w_ref, w_sems, tiles - len(w_parts))
    if stage == 0:
        acc[...] = jnp.zeros_like(acc)
    for copy in copies:
        copy.wait()

    def tile_step(tile, carry):
        new = ready(tile, pick, stage)
        if stage > 0:
            new = new & jnp.logical_not(ready(tile, pick, stage - 1))

        @pl.when(new)
        def _():
            add_tile(tile, pick, names, x_ref, w_ref, acc)

        return carry

    lax.fori_loop(0, tiles, tile_step, 0)


def early_kernel(stage, n_x, n_w, n_kept, pick, names, *refs):
    add_stage(stage, refs[:n_x], refs[n_x:n_x + n_w], pick, names, *refs[n_x + n_w + n_kept:])


def late_kernel(n_x, n_w, pick, names, up_ref, *refs):
    hidden_ref, grads_ref, *rest = refs[n_x + n_w + 3:]
    acc = rest[2]
    add_stage(2, refs[:n_x], refs[n_x:n_x + n_w], pick, names, *rest)
    for j in range(grads_ref.shape[0]):
        columns = slice(j * SIDE, (j + 1) * SIDE)
        gate = acc[j, :, :SIDE]
        up = acc[j, :, SIDE:]
        sig = 1.0 / (1.0 + jnp.exp(-gate))
        silu = gate * sig
        hidden_ref[:, columns] = (silu * up).astype(jnp.bfloat16)
        upstream = up_ref[:, columns].astype(jnp.float32)
        grads_ref[j, :, :SIDE] = (
            upstream * up * sig * (1.0 + gate * (1.0 - sig))
        ).astype(jnp.bfloat16)
        grads_ref[j, :, SIDE:] = (upstream * silu).astype(jnp.bfloat16)


def cost(tiles, slots, tokens, read, exps):
    return pl.CostEstimate(
        flops=2 * tiles * slots * tokens * SIDE * 2 * SIDE,
        bytes_accessed=read,
        transcendentals=exps,
    )


def forward_early(stage, pick, names, x_parts, w_parts, kept, col_count):
    tokens = kept[0].shape[1]
    parts = len(x_parts) + len(w_parts)
    return pl.pallas_call(
        functools.partial(early_kernel, stage, len(x_parts), len(w_parts), len(kept)),
        in_specs=[SCALARS] * 2 + [ANYWHERE] * parts + [ON_CHIP] * len(kept),
        out_specs=[ON_CHIP] * 3,
        out_shape=[pltpu.VMEM(array.shape, array.dtype) for array in kept[:2]] + [
            pltpu.VMEM((col_count + 1, tokens, 2 * SIDE), jnp.float32),
        ],
        input_output_aliases={2 + parts + number: number for number in range(len(kept))},
        scratch_shapes=[
            pltpu.SemaphoreType.DMA((len(x_parts),)),
            pltpu.SemaphoreType.DMA((len(w_parts),)),
        ],
        compiler_params=pltpu.CompilerParams(vmem_limit_bytes=VMEM_LIMIT),
        cost_estimate=cost(6 * (1 - stage), names.shape[1] // 2, tokens, 6 * (1 - stage) << 20, 0),
        name="forward_early",
    )(pick, names, *x_parts, *w_parts, *kept)


def forward_late(pick, names, upstream, x_parts, w_parts, x, w, acc):
    tokens, width = upstream.shape
    col_count = width // SIDE
    parts = len(x_parts) + len(w_parts)
    hidden, grads, _, w, _ = pl.pallas_call(
        functools.partial(late_kernel, len(x_parts), len(w_parts)),
        in_specs=[SCALARS] * 2 + [ON_CHIP] + [ANYWHERE] * parts + [ON_CHIP] * 3,
        out_specs=[ON_CHIP] * 5,
        out_shape=[
            jax.ShapeDtypeStruct((tokens, width), jnp.bfloat16),
            pltpu.VMEM((col_count, tokens, 2 * SIDE), jnp.bfloat16),
        ] + [pltpu.VMEM(kept.shape, kept.dtype) for kept in (x, w, acc)],
        input_output_aliases={3 + parts: 2, 4 + parts: 3, 5 + parts: 4},
        scratch_shapes=[
            pltpu.SemaphoreType.DMA((len(x_parts),)),
            pltpu.SemaphoreType.DMA((len(w_parts),)),
        ],
        compiler_params=pltpu.CompilerParams(vmem_limit_bytes=VMEM_LIMIT),
        cost_estimate=cost(len(w_parts) + 2, names.shape[1] // 2, tokens, 10 * upstream.size, 2 * upstream.size),
        name="forward_late",
    )(pick, names, upstream, *x_parts, *w_parts, x, w, acc)
    return hidden, grads, w


def backward_kernel(jobs, places, names, grads_ref, w_ref, *refs):
    slots = names.shape[1] // 2
    col_count = grads_ref.shape[0]
    outs = [k for k, _, _ in jobs]
    n_out = max(outs) + 1
    acc = refs[-1]
    added, outs = refs[:-1 - n_out], refs[-1 - n_out:-1]
    filled = [0] * n_out
    for k, position, sources in jobs:
        for j in range(3):
            columns = slice(j * SIDE, (j + 1) * SIDE)
            start = jnp.zeros(acc.shape[1:], jnp.float32)
            for number, part in sources:
                start += added[number][part, :, columns].astype(jnp.float32)
            acc[j] = start
        tile = places[position]
        for slot in range(slots):
            row = names[tile, slot]
            col = jnp.minimum(names[tile, slots + slot], col_count - 1)
            acc[row] += lax.dot_general(
                grads_ref[col],
                slot_of(w_ref, tile, slot),
                (((1,), (1,)), ((), ())),
                preferred_element_type=jnp.float32,
            )
        for j in range(3):
            outs[k][filled[k], :, j * SIDE:(j + 1) * SIDE] = acc[j].astype(outs[k].dtype)
        filled[k] += 1


def backward(jobs, added, places, names, grads, w, dtype):
    tokens = grads.shape[1]
    n_out = max(k for k, _, _ in jobs) + 1
    sizes = [sum(k == out for k, _, _ in jobs) for out in range(n_out)]
    return pl.pallas_call(
        functools.partial(backward_kernel, jobs),
        in_specs=[SCALARS] * 2 + [ON_CHIP] * (2 + len(added)),
        out_specs=[ON_CHIP] * n_out,
        out_shape=[jax.ShapeDtypeStruct((size, tokens, 3 * SIDE), dtype) for size in sizes],
        scratch_shapes=[pltpu.VMEM((4, tokens, SIDE), jnp.float32)],
        compiler_params=pltpu.CompilerParams(vmem_limit_bytes=VMEM_LIMIT),
        cost_estimate=cost(len(jobs), names.shape[1] // 2, tokens, 2 * len(jobs) * w.size // w.shape[0], 0),
        name="backward",
    )(places, names, grads, w, *added)


def after(value, *others):
    return lax.optimization_barrier((value,) + others)[0]


def gather(own, tokens, first):
    def swap(value):
        return shift(value, "core", 1)

    barrier = lax.optimization_barrier
    across = shift(tokens, "x_hi", 1)
    a1, t0 = turn(own, 1), swap(own)
    b1 = shift(after(own, t0), "x_lo", 1)
    a1, across, t0 = barrier((a1, across, t0))
    both = jnp.stack([tokens, across])
    a2 = turn(a1, 1)
    p1, m1 = shift(both, "z", 1), shift(both, "z", -1)
    t1 = swap(a1)
    a2, p1, m1, t1 = barrier((a2, p1, m1, t1))
    c1, a3, b2 = turn(b1, -1), turn(a2, 1), shift(a1, "x_lo", 1)
    kept = store((both, p1, m1), (own, t0, a1, t1, b1, a2), 0, 0)
    p2, m2 = shift(p1, "z", 1), shift(m1, "z", -1)
    p2, m2, kept = barrier((p2, m2, kept))
    p3, m3 = shift(p2, "z", 1), shift(m2, "z", -1)
    c2 = turn(c1, -1)
    b1, a2, p2, m2 = barrier((b1, a2, p2, m2))
    t2, t3 = swap(b1), swap(a2)
    known = (own, t0, a1, t1, b1, a2, c1, a3, b2)
    kept = first(kept, known, (p2, m2), (c1, a3, b2))
    p3, m3, c1, a3, b2, t2, t3, kept = barrier((p3, m3, c1, a3, b2, t2, t3, kept))
    t5, t6, t4 = swap(c1), swap(a3), swap(b2)
    p4, m4 = shift(p3[0], "z", 1), shift(m3[1], "z", -1)
    return kept, known, (p3, m3), (t2, t3, t5, t6, t4), (p4, m4), c2


def on_device(tokens, gate_blocks, up_blocks, block_row, block_col, upstream):
    table = lax.dynamic_slice_in_dim(jnp.asarray(PLANS), lax.axis_index(AXES), 1)[0]
    tokens, gate_blocks, table = lax.optimization_barrier((tokens, gate_blocks, table))
    pick, places = table[:16], table[16:]
    slots = gate_blocks.shape[0]
    i32, bf16 = jnp.int32, jnp.bfloat16
    ids = jnp.concatenate([
        jnp.where(block_row < 0, 3, block_row % 3),
        jnp.where(block_row < 0, 12, block_col % 12),
    ]).astype(bf16)
    ids = jnp.broadcast_to(jnp.pad(ids, (0, 2 * SIDE - 2 * slots))[None], (16, 2 * SIDE))
    blocks = jnp.concatenate([gate_blocks, up_blocks], axis=2).reshape(slots * SIDE, 2 * SIDE)
    line = lax.broadcasted_iota(i32, (16, 2 * slots), 0)

    def names_of(parts):
        names = jnp.zeros((16, 2 * slots), jnp.float32)
        for place, part in enumerate(parts):
            name = part[slots * SIDE:slots * SIDE + 1, :2 * slots].astype(jnp.float32)
            names = jnp.where(line == place, name, names)
        return names.astype(i32)

    col_count = upstream.shape[1] // SIDE

    def first(kept, known, x_parts, w_parts):
        return forward_early(0, pick, names_of(known), x_parts, w_parts, kept, col_count)

    kept, known, x_early, w_early, x_late, c2 = gather(jnp.concatenate([blocks, ids]), tokens, first)
    known += w_early
    x, w, acc = forward_early(1, pick, names_of(known), x_early, w_early, kept, col_count)
    c2, acc, x_late = lax.optimization_barrier((c2, acc, x_late))
    w_late = (c2, shift(c2, "core", 1))
    names = names_of(known + w_late)
    hidden, grads, w = forward_late(pick, names, upstream, x_late, w_late, x, w, acc)

    def share(jobs, added, dtype=bf16):
        return backward(jobs, added, places, names, grads, w, dtype)

    x4, x3 = share([(0, 0, ()), (1, 1, ()), (1, 2, ())], [])
    x4, x3 = shift(x4, "x_hi", 1), shift(x3, "x_hi", 1)
    plus, x2 = share([(0, 8, ((0, 0),)), (1, 3, ()), (1, 4, ())], [x4])
    plus, x2 = shift(plus, "z", 1), shift(x2, "x_hi", 1)
    plus, minus, x1 = share(
        [(0, 9, ((0, 0), (1, 0))), (1, 10, ((0, 1),)), (2, 5, ()), (2, 6, ())], [x3, plus])
    plus, minus, x1 = shift(plus, "z", 1), shift(minus, "z", -1), shift(x1, "x_hi", 1)
    plus, minus, x0 = share(
        [(0, 11, ((0, 0), (1, 0))), (1, 12, ((0, 1), (2, 0))), (2, 7, ())], [x2, plus, minus])
    plus, minus, x0 = shift(plus, "z", 1), shift(minus, "z", -1), shift(x0, "x_hi", 1)
    plus, minus = share(
        [(0, 13, ((0, 0), (1, 0))), (1, 14, ((0, 1), (2, 0)))], [x1, plus, minus])
    plus, minus = shift(plus, "z", 1), shift(minus, "z", -1)
    own, = share([(0, 15, ((0, 0),))], [x0], jnp.float32)
    grad_tokens = (own + plus.astype(jnp.float32) + minus.astype(jnp.float32)).astype(bf16)
    return hidden, grad_tokens[0]


def solution(mesh):
    fine = Mesh(mesh.devices.reshape([SIZES[a] for a in AXES]), AXES)
    both = P(ROW, COL)
    return jax.shard_map(
        on_device,
        mesh=fine,
        in_specs=(both, P(ROW + COL, None, None), P(ROW + COL, None, None), P(ROW + COL), P(ROW + COL), both),
        out_specs=(both, both),
        check_vma=False,
    )
```
